128 devices in a mesh: dp: 64 (over y, z, x), seq: 2 (over core).
Axes of the slice: x: 4, y: 4, z: 4, core: 2. Of those that a mesh axis runs over, the one named last changes fastest.
Arguments:
- tokens: bfloat16 [49152, 768], P(('dp', 'seq')), may hold values from -6 to 6
- cotangent: float32 [49152, 768], P(('dp', 'seq')), may hold values from -6 to 6
- doc_lengths: int32 [64, 4], P('dp'), may hold values from 1 to 512, 768 in all within a row
- timesteps: int32 [64, 4], P('dp'), may hold values from 0 to 999
- w_qkv: float32 [2304, 768], P(('dp', 'seq')), may hold values from -0.21875 to 0.21875
- w_out: float32 [768, 768], P(('dp', 'seq')), may hold values from -0.875 to 0.875
- w_up: float32 [3072, 768], P(('dp', 'seq')), may hold values from -0.21875 to 0.21875
- w_down: float32 [768, 3072], P(('dp', 'seq')), may hold values from -0.109375 to 0.109375
- w_ada: float32 [4608, 128], P(('dp', 'seq')), may hold values from -0.5 to 0.5
- row_qkv: float32 [2304], P(('dp', 'seq')), may hold values from 4423.68 to 17694.72
- col_qkv: float32 [768], replicated, may hold values from 4423.68 to 17694.72
- row_out: float32 [768], P(('dp', 'seq')), may hold values from 172.032 to 688.128
- col_out: float32 [768], replicated, may hold values from 172.032 to 688.128
- row_up: float32 [3072], P(('dp', 'seq')), may hold values from 368.64 to 1474.56
- col_up: float32 [768], replicated, may hold values from 368.64 to 1474.56
- row_down: float32 [768], P(('dp', 'seq')), may hold values from 1474.56 to 5898.24
- col_down: float32 [3072], replicated, may hold values from 1474.56 to 5898.24
- row_ada: float32 [4608], P(('dp', 'seq')), may hold values from 1966.08 to 7372.8
- col_ada: float32 [128], replicated, may hold values from 1966.08 to 7372.8
- norm_gains: float32 [2, 768], replicated, may hold values from 0.5 to 1.5
- gain_second: float32 [2, 768], replicated, may hold values from 983.04 to 45219.84
- biases: float32 [8448], replicated, may hold values from -1.25 to 1.25
- bias_second: float32 [8448], replicated, may hold values from 196.608 to 37355.52
Outputs:
- result: float32 [49152, 768], P(('dp', 'seq'))
- grad_tokens: float32 [49152, 768], P(('dp', 'seq'))
- grad_qkv: float32 [2304, 768], P(('dp', 'seq'))
- new_row_qkv: float32 [2304], P(('dp', 'seq'))
- new_col_qkv: float32 [768], replicated
- new_qkv: float32 [2304, 768], P(('dp', 'seq'))
- grad_out: float32 [768, 768], P(('dp', 'seq'))
- new_row_out: float32 [768], P(('dp', 'seq'))
- new_col_out: float32 [768], replicated
- new_out: float32 [768, 768], P(('dp', 'seq'))
- grad_up: float32 [3072, 768], P(('dp', 'seq'))
- new_row_up: float32 [3072], P(('dp', 'seq'))
- new_col_up: float32 [768], replicated
- new_up: float32 [3072, 768], P(('dp', 'seq'))
- grad_down: float32 [768, 3072], P(('dp', 'seq'))
- new_row_down: float32 [768], P(('dp', 'seq'))
- new_col_down: float32 [3072], replicated
- new_down: float32 [768, 3072], P(('dp', 'seq'))
- grad_ada: float32 [4608, 128], P(('dp', 'seq'))
- new_row_ada: float32 [4608], P(('dp', 'seq'))
- new_col_ada: float32 [128], replicated
- new_ada: float32 [4608, 128], P(('dp', 'seq'))
- grad_gains: float32 [2, 768], replicated
- new_gain_second: float32 [2, 768], replicated
- new_gains: float32 [2, 768], replicated
- grad_biases: float32 [8448], replicated
- new_bias_second: float32 [8448], replicated
- new_biases: float32 [8448], replicated
The draws below stay inside these ranges and needn't reach their ends.
Inputs may be any that keep to these rules, and one draw needn't show every extreme that they name: `doc_lengths`: each row sums to 768, and its longest sequence is exactly 512 rows.
All inputs are finite; a program needn't handle non-finite values.
Results may differ from the reference program's by a relative error of at most 0.012.
The reference program's roundings to bfloat16 on the way count: a program that leaves them out, or rounds other values in their place, can miss the bound.
Values may be sent and summed in bfloat16 or wider, within the bound.
A program may use at most 192 MiB of HBM per device.

```python
import math
import jax
import jax.numpy as jnp
import numpy as np
from jax import lax

D = 768
FF = 3072
HEADS = 12
HDIM = 64
COND = 128
TOK_DEV = 384
SLOTS = 4
STEP = 10
GROUPS = 64
GROUP_TOK = 768
LONGEST = 512
TOKENS = 49152
N_SEQ = 2


def draw_gain_second(key, part):
    key = jax.random.fold_in(key, 11)
    spread = jnp.exp(jax.random.uniform(key, (2, D), jnp.float32, 0.0, math.log(4.0)))
    level = jnp.concatenate([jnp.full((1, D), 0.23, jnp.float32), jnp.full((1, D), 0.02, jnp.float32)], axis=0)
    return level * float(TOKENS) * spread


def draw_bias_second(key, part):
    key = jax.random.fold_in(key, 17)
    spread = jnp.exp(jax.random.uniform(key, (FF + 7 * D,), jnp.float32, 0.0, math.log(4.0)))
    level = jnp.concatenate([jnp.full((FF,), 0.004, jnp.float32), jnp.full((D,), 0.05, jnp.float32), jnp.full((6 * D,), 0.19, jnp.float32)])
    return level * float(TOKENS) * spread


def with_ends(drawn, key, smallest, largest):
    spot = [jax.random.randint(jax.random.fold_in(key, axis), (), 0, length) for axis, length in enumerate(drawn.shape)]
    longest = drawn.shape.index(max(drawn.shape))
    neighbour = spot[:longest] + [(spot[longest] + 1) % drawn.shape[longest]] + spot[longest + 1:]
    return drawn.at[tuple(spot)].set(smallest).at[tuple(neighbour)].set(largest)


def level_of(key, shape, cuts, smallest, top_value):
    loudness = 1.0
    for dim, parts in cuts:
        steps = jax.random.uniform(jax.random.fold_in(jax.random.fold_in(key, 6), dim), (parts,), jnp.float32, smallest / len(cuts), top_value / len(cuts))
        loudness = loudness * jnp.repeat(jnp.exp(steps), shape[dim] // parts).reshape((-1,) + (1,) * (len(shape) - 1 - dim))
    return loudness


def profile(count, total, reach, lean):
    loads = [(1 << 20) // math.isqrt(rank ** lean) + 1 for rank in range(2, count + 1)]
    rest, holding = total - reach - (count - 1), [1] * (count - 1)
    while rest > 0:
        movable = [i for i in range(count - 1) if holding[i] < reach]
        whole, left = sum([loads[i] for i in movable]), rest
        for i in movable:
            extra = min(reach - holding[i], max(1, left * loads[i] // whole), rest)
            holding[i] = holding[i] + extra
            rest = rest - extra
    return np.array([reach] + holding)


def ragged(key, count, total, reach, skew):
    if count == 2:
        one = jax.random.randint(key, (), max(1, total - reach), min(reach, total - 1) + 1)
        return jnp.stack([one, total - one])
    sizes = jnp.asarray(profile(count, total, reach, skew), jnp.int32)
    twos = (count - 1) // 2
    source_of, taker = sizes[1:1 + 2 * twos:2], sizes[2:2 + 2 * twos:2]
    slack = jnp.minimum(source_of - 1, reach - taker)
    moved = jax.random.randint(jax.random.fold_in(key, 1), (twos,), 0, 1 << 20) % (slack + 1)
    sizes = sizes.at[1:1 + 2 * twos:2].set(source_of - moved).at[2:2 + 2 * twos:2].set(taker + moved)
    return sizes[jax.random.permutation(jax.random.fold_in(key, 2), count)]


def normal_values(stream_key, extent, scale, bound, cuts=(), held_as=jnp.bfloat16):
    values = scale * jax.random.normal(stream_key, extent, jnp.float32)
    if cuts:
        values = values * level_of(stream_key, extent, cuts, -0.22, 0.18)
    return jnp.clip(values, -bound, bound).astype(held_as)


def setup_inputs(seed: int = 0) -> dict:
    keys = jax.random.split(jax.random.key(seed), 24)
    tokens = normal_values(keys[0], (TOKENS, D), 1.0, 6.0, ((0, 128),))
    cotangent = normal_values(keys[1], (TOKENS, D), 1.0, 6.0, ((0, 128),), jnp.float32)
    doc_lengths = jax.vmap(lambda own: ragged(own, SLOTS, GROUP_TOK, LONGEST, 0))(jax.random.split(keys[2], GROUPS)).reshape((GROUPS, SLOTS)).astype(jnp.int32)
    timesteps = with_ends(jax.random.randint(keys[3], (GROUPS, SLOTS), 0, 1000), jax.random.fold_in(keys[3], 1), 0, 999).astype(jnp.int32)
    w_qkv = normal_values(keys[4], (3 * D, D), D ** -0.5, 0.21875, ((0, 128),), jnp.float32)
    w_out = normal_values(keys[5], (D, D), (D // 16) ** -0.5, 0.875, ((0, 128),), jnp.float32)
    w_up = normal_values(keys[6], (FF, D), D ** -0.5, 0.21875, ((0, 128),), jnp.float32)
    w_down = normal_values(keys[7], (D, FF), FF ** -0.5, 0.109375, ((0, 128),), jnp.float32)
    w_ada = normal_values(keys[8], (6 * D, COND), COND ** -0.5, 0.5, ((0, 128),), jnp.float32)
    row_qkv = jnp.clip(jnp.exp(math.log(17694.72) - 1.3862944 * jax.random.uniform(keys[9], (3 * D,), jnp.float32) ** level_of(keys[9], (3 * D,), ((0, 128),), -0.2, 0.2)), 4423.68, 17694.72)
    col_qkv = jnp.clip(jnp.exp(jax.random.uniform(keys[10], (D,), jnp.float32, math.log(4423.68), math.log(17694.72))), 4423.68, 17694.72)
    row_out = jnp.clip(jnp.exp(math.log(688.128) - 1.3862944 * jax.random.uniform(keys[11], (D,), jnp.float32) ** level_of(keys[11], (D,), ((0, 128),), -0.2, 0.2)), 172.032, 688.128)
    col_out = jnp.clip(jnp.exp(jax.random.uniform(keys[12], (D,), jnp.float32, math.log(172.032), math.log(688.128))), 172.032, 688.128)
    row_up = jnp.clip(jnp.exp(math.log(1474.56) - 1.3862944 * jax.random.uniform(keys[13], (FF,), jnp.float32) ** level_of(keys[13], (FF,), ((0, 128),), -0.2, 0.2)), 368.64, 1474.56)
    col_up = jnp.clip(jnp.exp(jax.random.uniform(keys[14], (D,), jnp.float32, math.log(368.64), math.log(1474.56))), 368.64, 1474.56)
    row_down = jnp.clip(jnp.exp(math.log(5898.24) - 1.3862944 * jax.random.uniform(keys[15], (D,), jnp.float32) ** level_of(keys[15], (D,), ((0, 128),), -0.2, 0.2)), 1474.56, 5898.24)
    col_down = jnp.clip(jnp.exp(jax.random.uniform(keys[16], (FF,), jnp.float32, math.log(1474.56), math.log(5898.24))), 1474.56, 5898.24)
    row_ada = jnp.clip(jnp.exp(math.log(7372.8) - 1.32175584 * jax.random.uniform(keys[17], (6 * D,), jnp.float32) ** level_of(keys[17], (6 * D,), ((0, 128),), -0.2, 0.2)), 1966.08, 7372.8)
    col_ada = jnp.clip(jnp.exp(jax.random.uniform(keys[18], (COND,), jnp.float32, math.log(1966.08), math.log(7372.8))), 1966.08, 7372.8)
    norm_gains = jnp.clip(1.0 + 0.1 * jax.random.normal(keys[19], (2, D), jnp.float32), 0.5, 1.5)
    gain_second = draw_gain_second(jax.random.fold_in(keys[23], 71), 0)
    biases = normal_values(keys[21], (FF + 7 * D,), 0.2, 1.25, (), jnp.float32)
    bias_second = draw_bias_second(jax.random.fold_in(keys[23], 71), 0)
    return {"tokens": tokens, "cotangent": cotangent, "doc_lengths": doc_lengths, "timesteps": timesteps, "w_qkv": w_qkv, "w_out": w_out, "w_up": w_up, "w_down": w_down, "w_ada": w_ada, "row_qkv": row_qkv, "col_qkv": col_qkv, "row_out": row_out, "col_out": col_out, "row_up": row_up, "col_up": col_up, "row_down": row_down, "col_down": col_down, "row_ada": row_ada, "col_ada": col_ada, "norm_gains": norm_gains, "gain_second": gain_second, "biases": biases, "bias_second": bias_second}


@jax.custom_vjp
def low(v):
    return lax.optimization_barrier(v.astype(jnp.bfloat16)).astype(jnp.float32)

@jax.custom_vjp
def low_back(v):
    return v

def low_keep(v):
    return (low(v), None)

def low_pass(kept, grad):
    return (grad,)

def back_keep(v):
    return (v, None)

def back_low(kept, grad):
    return (low(grad),)
low.defvjp(low_keep, low_pass)
low_back.defvjp(back_keep, back_low)
EPSILON = 1e-05
TINY_TERM = 1e-30
RELATIVE_RATE = 0.3
MASKED = -1e+30

def exact_dot(left, right):
    return jnp.dot(left, right, precision=lax.Precision.HIGHEST, preferred_element_type=jnp.float32)

def adaptive_norm(values, gain_vec, scale_mod, shift_mod):
    center = values - lax.optimization_barrier(jnp.mean(values, axis=-1, keepdims=True))
    spread = lax.optimization_barrier(jnp.mean(center * center, axis=-1, keepdims=True))
    normed = center * lax.rsqrt(spread + EPSILON)
    return normed * gain_vec * (1.0 + scale_mod) + shift_mod

def rotate(values, cosine, sine_part):
    half_dim = values.shape[-1] // 2
    turned = jnp.concatenate([-values[..., half_dim:], values[..., :half_dim]], axis=-1)
    return values * cosine + turned * sine_part

def rotary_tables(positions, head_width):
    inverse = jnp.exp(-math.log(10000.0) * jnp.arange(0, head_width, 2).astype(jnp.float32) / head_width)
    angles = positions.astype(jnp.float32)[:, None] * inverse[None, :]
    angles = jnp.concatenate([angles, angles], axis=-1)
    return (jnp.cos(angles)[:, None, :], jnp.sin(angles)[:, None, :])

def condition(step_ids, cond_width):
    half_dim = cond_width // 2
    frequency = jnp.exp(-math.log(10000.0) * jnp.arange(half_dim).astype(jnp.float32) / half_dim)
    angles = step_ids.astype(jnp.float32)[..., None] * frequency
    return jax.nn.silu(jnp.concatenate([jnp.cos(angles), jnp.sin(angles)], axis=-1))

def layout(lengths, group_rows):
    doc_ends = jnp.cumsum(lengths).astype(jnp.int32)
    starts = (doc_ends - lengths).astype(jnp.int32)
    row_ids = jnp.arange(group_rows).astype(jnp.int32)
    inside = (row_ids[:, None] >= starts[None, :]) & (row_ids[:, None] < doc_ends[None, :])
    member = inside.astype(jnp.float32)
    slot_ids = jnp.arange(lengths.shape[0]).astype(jnp.int32)
    doc_id = lax.optimization_barrier(jnp.sum(jnp.where(inside, slot_ids[None, :], 0), axis=1)).astype(jnp.int32)
    position = (row_ids - lax.optimization_barrier(jnp.sum(jnp.where(inside, starts[None, :], 0), axis=1))).astype(jnp.int32)
    return (member, doc_id, position)

def group_forward(x_group, lengths, cond_vec, wq, wo, wu, wd, wa, gains, bias_all):
    group_rows = x_group.shape[0]
    member, doc_id, position = layout(lengths, group_rows)
    mod_doc = exact_dot(low(cond_vec), low(wa).T) + bias_all[FF + D:]
    pieces = exact_dot(member, mod_doc).reshape(group_rows, 6, D)
    h_one = low(adaptive_norm(x_group, gains[0], pieces[:, 1], pieces[:, 0]))
    projected = low_back(exact_dot(h_one, low(wq).T)).reshape(group_rows, 3, HEADS, HDIM)
    cosine, sine_part = rotary_tables(position, HDIM)
    query = low(low_back(rotate(projected[:, 0], cosine, sine_part)))
    key_rot = low(low_back(rotate(projected[:, 1], cosine, sine_part)))
    value_low = low(projected[:, 2])
    raw = jnp.einsum('qhd,khd->hqk', query, key_rot, precision=lax.Precision.HIGHEST)
    same_doc = doc_id[:, None] == doc_id[None, :]
    logits = jnp.where(same_doc[None], low_back(raw * HDIM ** (-0.5)), MASKED)
    row_top = lax.optimization_barrier(jnp.max(logits, axis=-1, keepdims=True))
    exp_terms = jnp.exp(logits - row_top)
    attn_probs = exp_terms / lax.optimization_barrier(jnp.sum(exp_terms, axis=-1, keepdims=True))
    head_out = jnp.einsum('hqk,khd->qhd', low(attn_probs), value_low, precision=lax.Precision.HIGHEST)
    head_out = low(low_back(head_out.reshape(group_rows, D)))
    branch = low_back(exact_dot(head_out, low(wo).T))
    mid_state = x_group + pieces[:, 2] * branch
    h_two = low(adaptive_norm(mid_state, gains[1], pieces[:, 4], pieces[:, 3]))
    hidden_pre = low_back(exact_dot(h_two, low(wu).T) + bias_all[:FF])
    active = low(jax.nn.gelu(hidden_pre, approximate=True))
    mlp_out = low_back(exact_dot(active, low(wd).T) + bias_all[FF:FF + D])
    return mid_state + pieces[:, 5] * mlp_out

def factored_step(grad, master, row_old, col_old, decay_rate):
    square = grad * grad + TINY_TERM
    row_new = decay_rate * row_old + (1.0 - decay_rate) * lax.optimization_barrier(jnp.mean(square, axis=1))
    col_new = decay_rate * col_old + (1.0 - decay_rate) * lax.optimization_barrier(jnp.mean(square, axis=0))
    update = grad * lax.rsqrt(row_new / jnp.mean(row_new))[:, None] * lax.rsqrt(col_new)[None, :]
    update = update / jnp.maximum(1.0, jnp.sqrt(jnp.mean(update * update)))
    step_size = RELATIVE_RATE * jnp.maximum(0.001, jnp.sqrt(jnp.mean(master * master)))
    return (grad, row_new, col_new, master - step_size * update)

def plain_step(grad, master, second_old, decay_rate):
    second = decay_rate * second_old + (1.0 - decay_rate) * (grad * grad + TINY_TERM)
    update = grad * lax.rsqrt(second)
    update = update / jnp.maximum(1.0, jnp.sqrt(jnp.mean(update * update)))
    step_size = RELATIVE_RATE * jnp.maximum(0.001, jnp.sqrt(jnp.mean(master * master)))
    return (grad, second, master - step_size * update)

def reference(tokens, cotangent, doc_lengths, timesteps, w_qkv, w_out, w_up, w_down, w_ada, row_qkv, col_qkv, row_out, col_out, row_up, col_up, row_down, col_down, row_ada, col_ada, norm_gains, gain_second, biases, bias_second):
    decay_rate = 1.0 - float(STEP) ** (-0.8)
    group_rows = TOK_DEV * N_SEQ
    x_all = tokens.astype(jnp.float32).reshape(GROUPS, group_rows, D)
    conds = condition(timesteps, COND)
    checked = jax.checkpoint(group_forward)

    def forward(x_in, wq, wo, wu, wd, wa, gains, bias_all):

        def one_group(carry, items):
            x_group, lengths, cond_vec = items
            return (carry, checked(x_group, lengths, cond_vec, wq, wo, wu, wd, wa, gains, bias_all))
        _, outputs = lax.scan(one_group, jnp.zeros((), jnp.float32), (x_in, doc_lengths, conds))
        return outputs
    result, pullback = jax.vjp(forward, x_all, w_qkv, w_out, w_up, w_down, w_ada, norm_gains, biases)
    grads = pullback(cotangent.reshape(GROUPS, group_rows, D))
    qkv_out = factored_step(grads[1], w_qkv, row_qkv, col_qkv, decay_rate)
    out_out = factored_step(grads[2], w_out, row_out, col_out, decay_rate)
    up_out = factored_step(grads[3], w_up, row_up, col_up, decay_rate)
    down_out = factored_step(grads[4], w_down, row_down, col_down, decay_rate)
    ada_out = factored_step(grads[5], w_ada, row_ada, col_ada, decay_rate)
    gain_out = plain_step(grads[6], norm_gains, gain_second, decay_rate)
    bias_out = plain_step(grads[7], biases, bias_second, decay_rate)
    return (result.reshape(TOKENS, D), grads[0].reshape(TOKENS, D), qkv_out[0], qkv_out[1], qkv_out[2], qkv_out[3], out_out[0], out_out[1], out_out[2], out_out[3], up_out[0], up_out[1], up_out[2], up_out[3], down_out[0], down_out[1], down_out[2], down_out[3], ada_out[0], ada_out[1], ada_out[2], ada_out[3], gain_out[0], gain_out[1], gain_out[2], bias_out[0], bias_out[1], bias_out[2])
```

```python
import math

import jax
import jax.numpy as jnp
import numpy as np
from jax import lax
from jax.experimental import pallas as pl
from jax.experimental.pallas import tpu as pltpu
from jax.sharding import PartitionSpec as P

D = 768
FF = 3072
HEADS = 12
HDIM = 64
COND = 128
STEP = 10


EPSILON = 1e-05
TINY_TERM = 1e-30
RELATIVE_RATE = 0.3
MASKED = -1e30


def times_t(left, right):
    return lax.dot_general(
        left, right, (((1,), (1,)), ((), ())), preferred_element_type=jnp.float32
    )


def over_rows(left, right):
    return lax.dot_general(
        left, right, (((0,), (0,)), ((), ())), preferred_element_type=jnp.float32
    )


def exact_rows(left, right):
    return lax.dot_general(
        left,
        right,
        (((0,), (0,)), ((), ())),
        precision=lax.Precision.HIGHEST,
        preferred_element_type=jnp.float32,
    )


def adaptive_norm(values, gain_vec, scale_mod, shift_mod):
    center = values - jnp.mean(values, axis=-1, keepdims=True)
    spread = jnp.mean(center * center, axis=-1, keepdims=True)
    normed = center * lax.rsqrt(spread + EPSILON)
    return normed * gain_vec * (1.0 + scale_mod) + shift_mod


def rotate(values, cosine, sine_part):
    half_dim = values.shape[-1] // 2
    turned = jnp.concatenate([-values[..., half_dim:], values[..., :half_dim]], axis=-1)
    return values * cosine + turned * sine_part


def rotary_tables(positions, head_width):
    inverse = jnp.exp(
        -math.log(10000.0) * jnp.arange(0, head_width, 2).astype(jnp.float32) / head_width
    )
    angles = positions.astype(jnp.float32)[:, None] * inverse[None, :]
    angles = jnp.concatenate([angles, angles], axis=-1)
    return (jnp.cos(angles)[:, None, :], jnp.sin(angles)[:, None, :])


def condition(step_ids, cond_width):
    half_dim = cond_width // 2
    frequency = jnp.exp(-math.log(10000.0) * jnp.arange(half_dim).astype(jnp.float32) / half_dim)
    angles = step_ids.astype(jnp.float32)[..., None] * frequency
    return jax.nn.silu(jnp.concatenate([jnp.cos(angles), jnp.sin(angles)], axis=-1))


def layout(lengths, group_rows):
    doc_ends = jnp.cumsum(lengths)
    starts = doc_ends - lengths
    row_ids = jnp.arange(group_rows)
    inside = (row_ids[:, None] >= starts[None, :]) & (row_ids[:, None] < doc_ends[None, :])
    member = inside.astype(jnp.float32)
    slot_ids = jnp.arange(lengths.shape[0])
    doc_id = jnp.sum(jnp.where(inside, slot_ids[None, :], 0), axis=1)
    position = row_ids - jnp.sum(jnp.where(inside, starts[None, :], 0), axis=1)
    return (member, doc_id, position)


def head_scores(query, key_rot, same_doc):
    raw = times_t(query, key_rot)
    return jnp.where(same_doc, raw * query.shape[-1] ** (-0.5), MASKED)


MESH = pl.DeviceIdType.MESH
BF = jnp.bfloat16
F32 = jnp.float32
HALF = D // 2
LINE = {"qkv": 144, "out": 48, "up": 192, "down": 48, "ada": 288}
SHARD = {"qkv": 18, "out": 6, "up": 24, "down": 6, "ada": 36}


class Place:
    def __init__(self):
        spot = lax.axis_index("dp")
        self.core = lax.axis_index("seq")
        self.y = lax.div(spot, 16)
        self.z = lax.rem(lax.div(spot, 4), 4)
        self.x = lax.rem(spot, 4)
        self.line = 2 * self.x + self.core

    def at(self, y=None, z=None, x=None, core=None):
        y = self.y if y is None else y
        z = self.z if z is None else z
        x = self.x if x is None else x
        return (16 * y + 4 * z + x, self.core if core is None else core)

    def sibling(self):
        return self.at(core=1 - self.core)

    def along(self, axis, step):
        return self.at(**{axis: lax.rem(getattr(self, axis) + step, 4)})

    def on_line(self, step):
        other = lax.rem(self.line + step, 8)
        return other, self.at(x=lax.div(other, 2), core=lax.rem(other, 2))


class Net:
    def __init__(self, send, recv):
        self.send, self.recv, self.copies, self.arrived = send, recv, [], set()

    def put(self, src, dst, device):
        k = len(self.copies)
        copy = pltpu.make_async_remote_copy(
            src_ref=src,
            dst_ref=dst,
            send_sem=self.send.at[k],
            recv_sem=self.recv.at[k],
            device_id=device,
            device_id_type=MESH,
        )
        copy.start()
        self.copies.append(copy)
        return k

    def take(self, *keys):
        for k in keys:
            if k not in self.arrived:
                self.arrived.add(k)
                self.copies[k].wait_recv()

    def close(self):
        for k, copy in enumerate(self.copies):
            self.take(k)
            copy.wait_send()


def greet(devices):
    barrier = pltpu.get_barrier_semaphore()
    for device in devices:
        pl.semaphore_signal(barrier, inc=1, device_id=device, device_id_type=MESH)
    pl.semaphore_wait(barrier, len(devices))


def ring_gather(net, place, axis, view, split, share):
    me = getattr(place, axis)
    right, left = place.along(axis, 1), place.along(axis, 3)
    ahead, far, behind = (lax.rem(me + k, 4) for k in (1, 2, 3))

    def both(block):
        if share:
            net.put(block, block, place.sibling())

    go_right = net.put(view(me), view(me), right)
    go_left = net.put(view(me), view(me), left)
    both(view(me))
    yield
    net.take(go_right)
    first = split(view(behind), 0)
    on_right = net.put(first, first, right)
    both(view(behind))
    yield
    net.take(go_left)
    second = split(view(ahead), 1)
    on_left = net.put(second, second, left)
    both(view(ahead))
    yield
    net.take(on_right, on_left)
    both(view(far))


def add_to(out, *terms):
    total = terms[0][...].astype(F32)
    for term in terms[1:]:
        total = total + term[...].astype(F32)
    out[...] = total.astype(out.dtype)


def ring_reduce(net, place, axis, chunk, split, near, wide, out, add):
    me = getattr(place, axis)
    right, left = place.along(axis, 1), place.along(axis, 3)
    ahead, far, behind = (lax.rem(me + k, 4) for k in (1, 2, 3))
    far_right = net.put(split(chunk(far), 0), split(near[0], 0), right)
    far_left = net.put(split(chunk(far), 1), split(near[0], 1), left)
    plain_right = net.put(split(chunk(ahead), 1), split(wide[0], 1), right)
    plain_left = net.put(split(chunk(behind), 0), split(wide[1], 0), left)
    yield
    net.take(far_right)
    piece = split(chunk(ahead), 0)
    add(piece, piece, split(near[0], 0))
    sum_right = net.put(piece, split(wide[0], 0), right)
    yield
    net.take(far_left)
    piece = split(chunk(behind), 1)
    add(piece, piece, split(near[0], 1))
    sum_left = net.put(piece, split(wide[1], 1), left)
    yield
    net.take(plain_right, plain_left, sum_right, sum_left)
    add(out, chunk(me), wide[0], wide[1])


def run(flows):
    flows = list(flows)
    while flows:
        kept = []
        for flow in flows:
            try:
                next(flow)
                kept.append(flow)
            except StopIteration:
                pass
        flows = kept


def chain(*makers):
    for maker in makers:
        yield from maker()


def rows_split(first):
    def split(ref, half):
        total = ref.shape[-2]
        spot = pl.ds(0, first) if half == 0 else pl.ds(first, total - first)
        return ref.at[(slice(None),) * (len(ref.shape) - 2) + (spot,)]

    return split


def lead_split(ref, half):
    count = ref.shape[0] // 2
    return ref.at[pl.ds(half * count, count)]


def unit_tables():
    pick = np.zeros((576, 8 * 80), np.float32)
    for dev in range(8):
        for at, start, rows in ((0, 0, 18), (144, 18, 6), (192, 24, 24)):
            for j in range(rows):
                pick[at + dev * rows + j, dev * 80 + start + j] = 1
        for q in range(4):
            for j in range(6):
                pick[384 + 48 * q + dev * 6 + j, dev * 80 + 48 + 6 * q + j] = 1
    pick_ada = np.zeros((288, 8 * 48), np.float32)
    for dev in range(8):
        for j in range(36):
            pick_ada[dev * 36 + j, dev * 48 + j] = 1
    back = np.zeros((8 * 80, 432), np.float32)
    for dev in range(8):
        for at, start, rows in ((0, 0, 18), (144, 24, 6), (192, 32, 24), (384, 56, 6)):
            for j in range(rows):
                back[dev * 80 + start + j, at + dev * rows + j] = 1
    back_ada = np.zeros((3, 4 * 16, 144), np.float32)
    for part in range(3):
        for dev in range(4):
            for j in range(12):
                back_ada[part, dev * 16 + j, dev * 36 + part * 12 + j] = 1
    return [jnp.asarray(t, BF) for t in (pick, pick_ada, back, back_ada)]


def exact_pick(table, rows):
    return jnp.dot(table, rows, preferred_element_type=F32).astype(BF)


def gather_kernel(
    wq, wo, wu, wd, wa, pick, pick_ada, fq, fo, fu, fd, fa, pack, pack_ada, held, line, line_ada, send, recv
):
    place = Place()
    x, y, z, core = place.x, place.y, place.z, place.core
    net = Net(send, recv)
    cols = pl.ds(pl.multiple_of(core * HALF, 128), HALF)
    other = pl.ds(pl.multiple_of((1 - core) * HALF, 128), HALF)
    pack[72:80, :] = jnp.zeros((8, D), F32)
    pack[0:18, :] = wq[...]
    pack[18:24, :] = wo[...]
    pack[24:48, :] = wu[...]
    for q in range(4):
        pack[48 + 6 * q : 54 + 6 * q, :] = wd[:, q * D : (q + 1) * D]
    pack_ada[32:48, :] = jnp.zeros((16, COND), F32)
    pack_ada[0:36, :] = wa[...]
    line[x, core] = pack[:, cols].astype(BF)
    held[...] = pack[:, other].astype(BF)
    line_ada[x, core] = pack_ada[...].astype(BF)
    greet([place.sibling()] + [place.along(a, s) for a in ("x", "y", "z") for s in (1, 3)])
    swap = net.put(held, line.at[x, core], place.sibling())
    swap_ada = net.put(line_ada.at[x, core], line_ada.at[x, core], place.sibling())
    net.take(swap, swap_ada)
    run(
        [
            ring_gather(net, place, "x", lambda j: line_ada.at[j], lead_split, False),
            ring_gather(net, place, "x", lambda j: line.at[j], lead_split, False),
        ]
    )
    unit = line[...].reshape(640, HALF)
    ada_rows = pl.ds(pl.multiple_of(core * 144, 16), 144)
    fa[y, z, ada_rows, :] = exact_pick(pick_ada[ada_rows, :], line_ada[...].reshape(384, COND))
    fq[y, z, :, cols] = exact_pick(pick[0:144, :], unit)
    fo[y, z, :, cols] = exact_pick(pick[144:192, :], unit)
    fd[x, core, y, z] = exact_pick(pick[pl.ds(pl.multiple_of(384 + 48 * x, 16), 48), :], unit)
    fu[y, z, :, cols] = exact_pick(pick[192:384, :], unit)

    def z_then_y(block_z, block_y, first):
        return chain(
            lambda: ring_gather(net, place, "z", block_z, rows_split(first), False),
            lambda: ring_gather(net, place, "y", block_y, lead_split, True),
        )

    run(
        [
            z_then_y(lambda j: fa.at[y, j, ada_rows], lambda j: fa.at[j, :, ada_rows], 80),
            z_then_y(lambda j: fq.at[y, j, :, cols], lambda j: fq.at[j, :, :, cols], 80),
            z_then_y(lambda j: fo.at[y, j, :, cols], lambda j: fo.at[j, :, :, cols], 32),
            chain(
                lambda: ring_gather(net, place, "z", lambda j: fd.at[x, core, y, j], rows_split(32), False),
                lambda: ring_gather(net, place, "y", lambda j: fd.at[x, core, j], lead_split, False),
                lambda: ring_gather(net, place, "x", lambda j: fd.at[j, core], lead_split, True),
            ),
            chain(
                lambda: ring_gather(net, place, "y", lambda j: fu.at[j, z, :, cols], rows_split(96), False),
                lambda: ring_gather(net, place, "z", lambda j: fu.at[:, j, :, cols], lead_split, True),
            ),
        ]
    )
    net.close()


def gather_weights(wq, wo, wu, wd, wa, pick, pick_ada):
    vmem = pl.BlockSpec(memory_space=pltpu.VMEM)
    return pl.pallas_call(
        gather_kernel,
        out_shape=(
            jax.ShapeDtypeStruct((4, 4, 144, D), BF),
            jax.ShapeDtypeStruct((4, 4, 48, D), BF),
            jax.ShapeDtypeStruct((4, 4, 192, D), BF),
            jax.ShapeDtypeStruct((4, 2, 4, 4, 48, HALF), BF),
            jax.ShapeDtypeStruct((4, 4, 288, COND), BF),
        ),
        in_specs=[vmem] * 7,
        out_specs=[vmem] * 5,
        scratch_shapes=[
            pltpu.VMEM((80, D), F32),
            pltpu.VMEM((48, COND), F32),
            pltpu.VMEM((80, HALF), BF),
            pltpu.VMEM((4, 2, 80, HALF), BF),
            pltpu.VMEM((4, 2, 48, COND), BF),
            pltpu.SemaphoreType.DMA((96,)),
            pltpu.SemaphoreType.DMA((96,)),
        ],
        compiler_params=pltpu.CompilerParams(
            collective_id=1, has_side_effects=True, vmem_limit_bytes=56 << 20
        ),
    )(wq, wo, wu, wd, wa, pick, pick_ada)


def reduce_kernel(*refs):
    (
        sq, so, su, sd, sa, tq, to, tu, td, ta,
        wq, wo, wu, wd, wa, rq, ro, ru, rd, ra, cq, co, cu, cd, ca,
        gains, gain_second, biases, bias_second, small_in, back, back_ada,
    ) = refs[:32]
    outs = refs[32:58]
    (
        mq, mo, mu, md, ma, q1, o1, u1, d1, a1, d2, unit, unit_ada, dest, land, share,
        nq, no, nu, nd, na, nq2, no2, nu2, nd2, na2, nd3,
        wide_q, wide_o, wide_u, wide_d, wide_a, wide_q2, wide_o2, wide_u2, wide_d2, wide_a2, wide_d3,
        small, land_x, land_z, land_y, part, done, send, recv,
    ) = refs[58:]
    place = Place()
    x, y, z, core, line = place.x, place.y, place.z, place.core, place.line
    net = Net(send, recv)
    peers = [place.on_line(k)[1] for k in range(1, 8)]
    peers += [place.along(a, k) for a in ("y", "z") for k in (1, 2, 3)]
    greet(peers)
    sent = [
        net.put(src, dst, place.sibling())
        for src, dst in ((sd, md), (su, mu), (so, mo), (sq, mq), (sa, ma))
    ]
    for key, own, got in zip(sent, (td, tu, to, tq, ta), (md, mu, mo, mq, ma)):
        net.take(key)
        for j in range(4):

            @pl.loop(0, 4)
            def _(k):
                add_to(got.at[j, k], own.at[j, k], got.at[j, k])

    def each(out, *terms):
        if len(out.shape) == 2:
            add_to(out, *terms)
        elif len(out.shape) == 3:
            for j in range(out.shape[0]):
                add_to(out.at[j], *(t.at[j] for t in terms))
        else:
            for j in range(out.shape[0]):

                @pl.loop(0, out.shape[1])
                def _(k):
                    add_to(out.at[j, k], *(t.at[j, k] for t in terms))

    def reduce(axis, chunk, split, near, wide, out):
        return lambda: ring_reduce(
            net, place, axis, chunk, split, (near,), (wide.at[0], wide.at[1]), out, each
        )

    run(
        [
            chain(
                reduce("x", lambda j: md.at[j], lead_split, nd, wide_d, d1),
                reduce("y", lambda j: d1.at[j], lead_split, nd2, wide_d2, d2),
                reduce("z", lambda j: d2.at[j], rows_split(32), nd3, wide_d3, unit.at[pl.ds(384, 48)]),
            ),
            chain(
                reduce("z", lambda j: mu.at[:, j], lead_split, nu, wide_u, u1),
                reduce("y", lambda j: u1.at[j], rows_split(96), nu2, wide_u2, unit.at[pl.ds(192, 192)]),
            ),
            chain(
                reduce("y", lambda j: mo.at[j], lead_split, no, wide_o, o1),
                reduce("z", lambda j: o1.at[j], rows_split(32), no2, wide_o2, unit.at[pl.ds(144, 48)]),
            ),
            chain(
                reduce("y", lambda j: mq.at[j], lead_split, nq, wide_q, q1),
                reduce("z", lambda j: q1.at[j], rows_split(80), nq2, wide_q2, unit.at[pl.ds(0, 144)]),
            ),
            chain(
                reduce("y", lambda j: ma.at[j], lead_split, na, wide_a, a1),
                reduce("z", lambda j: a1.at[j], rows_split(80), na2, wide_a2, unit_ada),
            ),
        ]
    )
    dest[...] = exact_pick(back[...], unit[...]).reshape(8, 80, HALF)
    for part_no in range(3):
        moved = exact_pick(back_ada[part_no], unit_ada[...]).reshape(4, 16, COND)
        dest[pl.ds(4 * core, 4), 64:80, part_no * COND : (part_no + 1) * COND] = moved
    keys = []
    for k in range(1, 8):
        other, device = place.on_line(k)
        keys.append(net.put(dest.at[other], land.at[line], device))
    land[line] = dest[line]
    net.take(*keys)
    for half in range(2):
        total = land[half, 0:56, :].astype(F32)
        for j in range(1, 4):
            total = total + land[2 * j + half, 0:56, :].astype(F32)
        share[0:56, half * HALF : (half + 1) * HALF] = total
    own_core = lax.div(line, 4)
    total = land[own_core, 64:80, :].astype(F32)
    for j in range(1, 4):
        total = total + land[2 * j + own_core, 64:80, :].astype(F32)
    share[56:72, 0:HALF] = total
    grad_down = jnp.concatenate(
        [land[j, 56:64, :].astype(F32) for j in range(8)], axis=1
    )[0:6]
    grad_ada = jnp.concatenate(
        [share[56:68, j * COND : (j + 1) * COND] for j in range(3)], axis=0
    )
    grads = (share[0:18, :], share[24:30, :], share[32:56, :], grad_down, grad_ada)
    finish(
        place, net, grads, (wq, wo, wu, wd, wa), (rq, ro, ru, rd, ra), (cq, co, cu, cd, ca),
        gains, gain_second, biases, bias_second, small_in, small, land_x, land_z, land_y, part, done, outs,
    )
    net.close()


def piece_of(ref, number):
    rows = pl.ds(pl.multiple_of(8 * lax.div(number, 2), 8), 8)
    return ref.at[rows, pl.ds(pl.multiple_of(HALF * lax.rem(number, 2), 128), HALF)]


def finish(
    place, net, grads, masters, rows_old, cols_old, gains, gain_second, biases, bias_second,
    small_in, small, land_x, land_z, land_y, part, done, outs,
):
    decay = 1.0 - float(STEP) ** (-0.8)
    counts = (3 * D, D, FF, D, 6 * D)
    widths = (D, D, D, FF, COND)
    col_at = (13, 14, 15, 16, 20)
    ratio_at = (21, 22, 23, 24, 28)
    small[0:13, :] = small_in[0:13, :]
    small[13:32, :] = jnp.zeros((19, D), F32)
    lanes = lax.broadcasted_iota(jnp.int32, (1, D), 1)
    totals = jnp.zeros((1, D), F32)

    def whole(values):
        return jnp.sum(jnp.sum(values, axis=1, keepdims=True), axis=0, keepdims=True)

    rows_new = []
    for n in range(5):
        grad = grads[n]
        square = grad * grad
        row_new = decay * rows_old[n][...] + (1.0 - decay) * jnp.mean(
            square + TINY_TERM, axis=1, keepdims=True
        )
        rows_new.append(row_new)
        outs[4 * n][...] = grad
        outs[4 * n + 1][...] = row_new
        col_sum = jnp.sum(square + TINY_TERM, axis=0, keepdims=True)
        ratio = jnp.sum(square / row_new, axis=0, keepdims=True)
        if widths[n] == COND:
            small[col_at[n] : col_at[n] + 1, 0:COND] = col_sum
            small[ratio_at[n] : ratio_at[n] + 1, 0:COND] = ratio
        else:
            for q in range(widths[n] // D):
                small[col_at[n] + q : col_at[n] + q + 1, :] = col_sum[:, q * D : (q + 1) * D]
                small[ratio_at[n] + q : ratio_at[n] + q + 1, :] = ratio[:, q * D : (q + 1) * D]
        master = masters[n][...]
        totals = totals + jnp.where(lanes == n, whole(row_new), 0.0)
        totals = totals + jnp.where(lanes == 5 + n, whole(master * master), 0.0)
    small[29:30, :] = totals

    me = place.line
    keys = []
    for k in range(1, 8):
        other, device = place.on_line(k)
        keys.append(net.put(piece_of(small, other), land_x.at[me], device))
    land_x[me] = piece_of(small, me)[...]
    net.take(*keys)
    stage = 0
    part[0] = sum((land_x[j] for j in range(1, 8)), start=land_x[0])
    for axis, land in (("z", land_z), ("y", land_y)):
        spot = getattr(place, axis)
        keys = [net.put(part.at[stage], land.at[spot], place.along(axis, k)) for k in (1, 2, 3)]
        land[spot] = part[stage]
        net.take(*keys)
        stage += 1
        part[stage] = sum((land[j] for j in range(1, 4)), start=land[0])
    keys = [net.put(part.at[stage], piece_of(done, me), place.on_line(k)[1]) for k in range(1, 8)]
    piece_of(done, me)[...] = part[stage]
    net.take(*keys)

    totals = done[29:30, :]

    def scalar(n):
        return jnp.sum(jnp.where(lanes == n, totals, 0.0), axis=1, keepdims=True)

    for n in range(5):
        entries = counts[n] * widths[n]
        if widths[n] == COND:
            col_sum = done[col_at[n] : col_at[n] + 1, 0:COND]
            ratio = done[ratio_at[n] : ratio_at[n] + 1, 0:COND]
        else:
            across = range(widths[n] // D)
            col_sum = jnp.concatenate([done[col_at[n] + q : col_at[n] + q + 1, :] for q in across], axis=1)
            ratio = jnp.concatenate([done[ratio_at[n] + q : ratio_at[n] + q + 1, :] for q in across], axis=1)
        col_new = decay * cols_old[n][...] + (1.0 - decay) * (col_sum / counts[n])
        row_mean = scalar(n) / counts[n]
        square_sum = row_mean * jnp.sum(ratio / col_new, axis=1, keepdims=True)
        clip = jnp.maximum(1.0, jnp.sqrt(square_sum / entries))
        size = RELATIVE_RATE * jnp.maximum(0.001, jnp.sqrt(scalar(5 + n) / entries))
        update = grads[n] * lax.rsqrt(rows_new[n] / row_mean) * lax.rsqrt(col_new)
        outs[4 * n + 2][...] = col_new
        outs[4 * n + 3][...] = masters[n][...] - update * (size / clip)
    for at, rows, master, second_old, base in ((0, 2, gains, gain_second, 20), (2, 11, biases, bias_second, 23)):
        grad = done[at : at + rows, :]
        second = decay * second_old[...] + (1.0 - decay) * (grad * grad + TINY_TERM)
        update = grad * lax.rsqrt(second)
        size = float(rows * D)
        clip = jnp.maximum(1.0, jnp.sqrt(whole(update * update) / size))
        old = master[...]
        step = RELATIVE_RATE * jnp.maximum(0.001, jnp.sqrt(whole(old * old) / size))
        outs[base][...] = grad
        outs[base + 1][...] = second
        outs[base + 2][...] = old - update * (step / clip)


def reduce_and_step(sides, owns, masters, rows_old, cols_old, gains, gain_second, biases, bias_second, small, tables):
    vmem = pl.BlockSpec(memory_space=pltpu.VMEM)
    shapes = []
    for master, col in zip(masters, cols_old):
        rows = master.shape[0]
        shapes += [master.shape, (rows, 1), col.shape, master.shape]
    shapes += [gains.shape] * 3 + [biases.shape] * 3
    operands = (*sides, *owns, *masters, *rows_old, *cols_old, gains, gain_second, biases, bias_second, small, *tables)
    half = [pltpu.VMEM(s.shape, BF) for s in sides]
    mats = (half[2], half[1], half[1], half[3], half[4])
    scratch = [pltpu.VMEM(s.shape, BF) for s in sides]
    scratch += [
        pltpu.VMEM((4, 144, HALF), BF), pltpu.VMEM((4, 48, HALF), BF), pltpu.VMEM((4, 192, HALF), BF),
        pltpu.VMEM((4, 4, 48, HALF), BF), pltpu.VMEM((4, 144, COND), BF), pltpu.VMEM((4, 48, HALF), BF),
        pltpu.VMEM((432, HALF), BF), pltpu.VMEM((144, COND), BF),
        pltpu.VMEM((8, 80, HALF), BF), pltpu.VMEM((8, 80, HALF), BF), pltpu.VMEM((72, D), F32),
    ]
    first = [(4, 144, HALF), (4, 48, HALF), (4, 192, HALF), (4, 4, 48, HALF), (4, 144, COND)]
    then = [(144, HALF), (48, HALF), (192, HALF), (4, 48, HALF), (144, COND), (48, HALF)]
    scratch += [pltpu.VMEM(s, BF) for s in first + then]
    scratch += [pltpu.VMEM((2,) + s, BF) for s in first + then]
    scratch += [
        pltpu.VMEM((32, D), F32), pltpu.VMEM((8, 8, HALF), F32), pltpu.VMEM((4, 8, HALF), F32),
        pltpu.VMEM((4, 8, HALF), F32), pltpu.VMEM((3, 8, HALF), F32), pltpu.VMEM((32, D), F32),
        pltpu.SemaphoreType.DMA((112,)), pltpu.SemaphoreType.DMA((112,)),
    ]
    return pl.pallas_call(
        reduce_kernel,
        out_shape=tuple(jax.ShapeDtypeStruct(s, F32) for s in shapes),
        in_specs=[vmem] * len(operands),
        out_specs=[vmem] * len(shapes),
        scratch_shapes=scratch,
        compiler_params=pltpu.CompilerParams(
            collective_id=2, has_side_effects=True, vmem_limit_bytes=56 << 20
        ),
    )(*operands)


def local(
    tokens,
    cotangent,
    doc_lengths,
    timesteps,
    w_qkv,
    w_out,
    w_up,
    w_down,
    w_ada,
    row_qkv,
    col_qkv,
    row_out,
    col_out,
    row_up,
    col_up,
    row_down,
    col_down,
    row_ada,
    col_ada,
    norm_gains,
    gain_second,
    biases,
    bias_second,
):
    seq_count = lax.axis_size("seq")
    seq_rank = lax.axis_index("seq")
    local_rows = tokens.shape[0]
    group_rows = local_rows * seq_count
    head_group = HEADS // seq_count
    part_width = D // seq_count
    pick, pick_ada, back, back_ada = unit_tables()
    full_qkv, full_out, full_up, full_down, full_ada = gather_weights(
        w_qkv, w_out, w_up, w_down, w_ada, pick, pick_ada
    )
    full_qkv = full_qkv.reshape(3 * D, D)
    full_out = full_out.reshape(D, D)
    full_up = full_up.reshape(FF, D)
    full_down = full_down.transpose(2, 3, 4, 0, 1, 5).reshape(D, FF)
    full_ada = full_ada.reshape(6 * D, COND)
    member, doc_id, position = layout(doc_lengths[0], group_rows)
    row_start = seq_rank * local_rows
    member_local = lax.dynamic_slice_in_dim(member, row_start, local_rows, 0)
    position_local = lax.dynamic_slice_in_dim(position, row_start, local_rows, 0)
    cond_vec = condition(timesteps[0], COND).astype(jnp.bfloat16)
    bias_up = biases[:FF]
    bias_down = biases[FF : FF + D]
    mod_doc = times_t(cond_vec, full_ada) + biases[FF + D :]
    pieces = jnp.dot(
        member_local, mod_doc, precision=lax.Precision.HIGHEST, preferred_element_type=jnp.float32
    ).reshape(local_rows, 6, D)
    gain_one = norm_gains[0]
    gain_two = norm_gains[1]
    values = tokens.astype(jnp.float32)
    h_one = adaptive_norm(values, gain_one, pieces[:, 1], pieces[:, 0]).astype(jnp.bfloat16)
    triple = times_t(h_one, full_qkv).reshape(local_rows, 3, HEADS, HDIM)
    cosine, sine_part = rotary_tables(position_local, HDIM)
    query_rot = rotate(triple[:, 0], cosine, sine_part).astype(jnp.bfloat16)
    key_rot = rotate(triple[:, 1], cosine, sine_part).astype(jnp.bfloat16)
    value_low = triple[:, 2].astype(jnp.bfloat16)
    packed = jnp.stack([query_rot, key_rot, value_low]).reshape(
        3, local_rows, seq_count, part_width
    )
    head_block = lax.all_to_all(packed, "seq", split_axis=2, concat_axis=1, tiled=True)
    query_h = jnp.moveaxis(head_block[0].reshape(group_rows, head_group, HDIM), 1, 0)
    key_h = jnp.moveaxis(head_block[1].reshape(group_rows, head_group, HDIM), 1, 0)
    value_h = jnp.moveaxis(head_block[2].reshape(group_rows, head_group, HDIM), 1, 0)
    same_doc = doc_id[:, None] == doc_id[None, :]

    def head_forward(operands):
        query_one, key_one, value_one = operands
        logits = head_scores(query_one, key_one, same_doc)
        row_top = jnp.max(logits, axis=-1, keepdims=True)
        exp_terms = jnp.exp(logits - row_top)
        row_total = jnp.sum(exp_terms, axis=-1, keepdims=True)
        probs_low = (exp_terms / row_total).astype(jnp.bfloat16)
        out_one = jnp.dot(probs_low, value_one, preferred_element_type=jnp.float32)
        return (out_one.astype(jnp.bfloat16), row_top + jnp.log(row_total))

    head_low, log_total = lax.map(head_forward, (query_h, key_h, value_h))
    head_low = jnp.moveaxis(head_low, 0, 1).reshape(group_rows, 1, part_width)
    token_out = lax.all_to_all(head_low, "seq", split_axis=0, concat_axis=1, tiled=True)
    attended = token_out.reshape(local_rows, D)
    branch = times_t(attended, full_out)
    gate_one = pieces[:, 2]
    mid_state = values + gate_one * branch
    h_two = adaptive_norm(mid_state, gain_two, pieces[:, 4], pieces[:, 3]).astype(jnp.bfloat16)
    hidden_pre = times_t(h_two, full_up) + bias_up
    active = jax.nn.gelu(hidden_pre, approximate=True).astype(jnp.bfloat16)
    mlp_out = times_t(active, full_down) + bias_down
    gate_two = pieces[:, 5]
    result = mid_state + gate_two * mlp_out
    grad_mlp = (gate_two * cotangent).astype(jnp.bfloat16)
    grad_gate_two = cotangent * mlp_out
    grad_b_down = jnp.sum(grad_mlp, axis=0, dtype=jnp.float32)
    grad_active = jnp.dot(grad_mlp, full_down, preferred_element_type=jnp.float32)
    _, gelu_back = jax.vjp(lambda pre: jax.nn.gelu(pre, approximate=True), hidden_pre)
    grad_hidden = gelu_back(grad_active)[0].astype(jnp.bfloat16)
    grad_b_up = jnp.sum(grad_hidden, axis=0, dtype=jnp.float32)
    grad_h_two = jnp.dot(grad_hidden, full_up, preferred_element_type=jnp.float32)
    _, norm_back_two = jax.vjp(adaptive_norm, mid_state, gain_two, pieces[:, 4], pieces[:, 3])
    grad_mid_norm, grad_g_two, grad_scale_two, grad_shift_two = norm_back_two(grad_h_two)
    grad_mid = cotangent + grad_mid_norm
    grad_gate_one = grad_mid * branch
    grad_branch = (gate_one * grad_mid).astype(jnp.bfloat16)
    grad_attended = jnp.dot(grad_branch, full_out, preferred_element_type=jnp.float32).astype(
        jnp.bfloat16
    )
    grad_heads = lax.all_to_all(
        grad_attended.reshape(local_rows, seq_count, part_width),
        "seq",
        split_axis=1,
        concat_axis=0,
        tiled=True,
    )
    grad_head_out = jnp.moveaxis(grad_heads.reshape(group_rows, head_group, HDIM), 1, 0)
    score_scale = HDIM ** (-0.5)

    def head_backward(operands):
        query_one, key_one, value_one, grad_one, lse_one = operands
        logits = head_scores(query_one, key_one, same_doc)
        attn_probs = jnp.exp(logits - lse_one)
        probs_low = attn_probs.astype(jnp.bfloat16)
        grad_value = over_rows(probs_low, grad_one)
        grad_probs = times_t(grad_one, value_one)
        shared_term = jnp.sum(grad_probs * attn_probs, axis=-1, keepdims=True)
        grad_logits = (attn_probs * (grad_probs - shared_term)).astype(jnp.bfloat16)
        grad_query = jnp.dot(grad_logits, key_one, preferred_element_type=jnp.float32) * score_scale
        grad_key = over_rows(grad_logits, query_one) * score_scale
        return (
            grad_query.astype(jnp.bfloat16),
            grad_key.astype(jnp.bfloat16),
            grad_value.astype(jnp.bfloat16),
        )

    grad_q_h, grad_k_h, grad_v_h = lax.map(
        head_backward, (query_h, key_h, value_h, grad_head_out, log_total)
    )
    grad_pack = jnp.stack(
        [jnp.moveaxis(grad_q_h, 0, 1), jnp.moveaxis(grad_k_h, 0, 1), jnp.moveaxis(grad_v_h, 0, 1)]
    ).reshape(3, group_rows, 1, part_width)
    grad_local = lax.all_to_all(grad_pack, "seq", split_axis=1, concat_axis=2, tiled=True)
    grad_local = grad_local.reshape(3, local_rows, HEADS, HDIM)
    _, rotate_back = jax.vjp(lambda part: rotate(part, cosine, sine_part), triple[:, 0])
    grad_q_plain = rotate_back(grad_local[0].astype(jnp.float32))[0]
    grad_k_plain = rotate_back(grad_local[1].astype(jnp.float32))[0]
    grad_projected = jnp.stack(
        [grad_q_plain.astype(jnp.bfloat16), grad_k_plain.astype(jnp.bfloat16), grad_local[2]],
        axis=1,
    ).reshape(local_rows, 3 * D)
    grad_h_one = jnp.dot(grad_projected, full_qkv, preferred_element_type=jnp.float32)
    _, norm_back_one = jax.vjp(adaptive_norm, values, gain_one, pieces[:, 1], pieces[:, 0])
    grad_in_norm, grad_g_one, grad_scale_one, grad_shift_one = norm_back_one(grad_h_one)
    grad_tokens = grad_mid + grad_in_norm
    grad_pieces = jnp.stack(
        [
            grad_shift_one,
            grad_scale_one,
            grad_gate_one,
            grad_shift_two,
            grad_scale_two,
            grad_gate_two,
        ],
        axis=1,
    ).reshape(local_rows, 6 * D)
    grad_mod_doc = exact_rows(member_local, grad_pieces)
    grad_w_ada = exact_rows(grad_mod_doc, cond_vec.astype(jnp.float32))
    grad_b_ada = jnp.sum(grad_mod_doc, axis=0)
    def halves(left, right):
        def one(which):
            part = lax.dynamic_slice_in_dim(right, which * HALF, HALF, 1)
            grad = over_rows(left, part).astype(BF)
            return grad.reshape(4, 4, grad.shape[0] // 16, HALF)

        return one(1 - seq_rank), one(seq_rank)

    def halves_down(which):
        cut = lax.dynamic_slice_in_dim(active.reshape(local_rows, 4, 2, HALF), which, 1, 2)
        grad = over_rows(grad_mlp, cut.reshape(local_rows, 4 * HALF)).astype(BF)
        return jnp.moveaxis(grad.reshape(4, 4, 48, 4, HALF), 3, 0)

    def halves_ada(which):
        cut = grad_w_ada.astype(BF).reshape(4, 4, 2, 144, COND)
        return lax.dynamic_index_in_dim(cut, which, 2, False)

    pairs = (
        halves(grad_projected, h_one),
        halves(grad_branch, attended),
        halves(grad_hidden, h_two),
        (halves_down(1 - seq_rank), halves_down(seq_rank)),
        (halves_ada(1 - seq_rank), halves_ada(seq_rank)),
    )
    small = jnp.concatenate(
        [grad_g_one, grad_g_two, grad_b_up, grad_b_down, grad_b_ada, jnp.zeros((19 * D,), F32)]
    ).reshape(32, D)
    stepped = reduce_and_step(
        [p[0] for p in pairs],
        [p[1] for p in pairs],
        (w_qkv, w_out, w_up, w_down, w_ada),
        [r[:, None] for r in (row_qkv, row_out, row_up, row_down, row_ada)],
        [c[None, :] for c in (col_qkv, col_out, col_up, col_down, col_ada)],
        norm_gains,
        gain_second,
        biases.reshape(11, D),
        bias_second.reshape(11, D),
        small,
        (back, back_ada),
    )
    outputs = [result, grad_tokens]
    for n in range(5):
        outputs += [stepped[4 * n], stepped[4 * n + 1][:, 0], stepped[4 * n + 2][0], stepped[4 * n + 3]]
    outputs += list(stepped[20:23]) + [s.reshape(-1) for s in stepped[23:26]]
    return tuple(outputs)


def solution(mesh):
    placed = (
        P(("dp", "seq"), None),
        P(("dp", "seq"), None),
        P("dp", None),
        P("dp", None),
        P(("dp", "seq"), None),
        P(("dp", "seq"), None),
        P(("dp", "seq"), None),
        P(("dp", "seq"), None),
        P(("dp", "seq"), None),
        P(("dp", "seq")),
        P(),
        P(("dp", "seq")),
        P(),
        P(("dp", "seq")),
        P(),
        P(("dp", "seq")),
        P(),
        P(("dp", "seq")),
        P(),
        P(),
        P(),
        P(),
        P(),
    )
    return jax.shard_map(
        local,
        mesh=mesh,
        in_specs=placed,
        out_specs=(
            P(("dp", "seq"), None),
            P(("dp", "seq"), None),
            P(("dp", "seq"), None),
            P(("dp", "seq")),
            P(),
            P(("dp", "seq"), None),
            P(("dp", "seq"), None),
            P(("dp", "seq")),
            P(),
            P(("dp", "seq"), None),
            P(("dp", "seq"), None),
            P(("dp", "seq")),
            P(),
            P(("dp", "seq"), None),
            P(("dp", "seq"), None),
            P(("dp", "seq")),
            P(),
            P(("dp", "seq"), None),
            P(("dp", "seq"), None),
            P(("dp", "seq")),
            P(),
            P(("dp", "seq"), None),
            P(),
            P(),
            P(),
            P(),
            P(),
            P(),
        ),
        check_vma=False,
    )
```
